512 devices in a mesh: dom: 32 (over x, z), bal: 16 (over y, core).
Axes of the slice: x: 4, y: 8, z: 8, core: 2. Of those that a mesh axis runs over, the one named last changes fastest.
Arguments:
- edge_wind: bfloat16 [55, 1572864], P(None, ('dom', 'bal')), may hold values from -6 to 6
- send_edges: int32 [2, 131072], P(None, ('dom', 'bal')), may hold values from 0 to 3071, as said below
- stencil: int32 [10, 524288], P(None, ('dom', 'bal')), may hold values from 0 to 3581, as said below
- rbf_coeff: float32 [2, 10, 524288], P(None, None, ('dom', 'bal')), may hold values from -2 to 2
- state: float32 [4, 55, 524288], P(None, None, ('dom', 'bal')), may hold values from 0 to 2
- rain_cols: int32 [262144], P(('dom', 'bal')), may hold values from 0 to 1023, as said below
- rain_count: int32 [512], P(('dom', 'bal')), may hold values from 0 to 512, as said below
Outputs:
- cell_wind: bfloat16 [2, 55, 524288], P(None, None, ('dom', 'bal'))
- tendency: float32 [4, 55, 524288], P(None, None, ('dom', 'bal'))
The draws below stay inside these ranges and needn't reach their ends.
Inputs may be any that keep to these rules, and one draw needn't show every extreme that they name: `send_edges`: entries are own edge numbers of the sending partition. `stencil`: numbers index the extended edge list of the cell's partition: 256 received from the preceding partition along dom, its own 3072, then 256 from the following one. The entries of local cell n lie between 3 n and 3 n + 512. `rain_cols`: each partition's block holds distinct local cell numbers; entries at and beyond its count are unused. `rain_count`: two partitions whose bal indices differ only in the lowest bit hold exactly 512 precipitating cells together.
All inputs are finite; a program needn't handle non-finite values.
Results may differ from the reference program's by a relative error of at most 0.0065.
Values may be sent and summed in bfloat16 or wider, within the bound.
No kernel may reach another device: no remote copies, remote signals or barrier semaphores. Data moves between devices by JAX's collectives and lax.ppermute only.
A program may use at most 64 MiB of HBM per device.

```python
import math
import jax
import jax.numpy as jnp

LEV = 55
CELLS = 1024
NSTEN = 10
NSUB = 3
EDGES = 3072
HALO = 256
RAIN_MAX = 512
PARTITIONS = 512
GROUPS = 32
PAIRS_GROUP = 8
TOTAL_CELLS = 524288
TOTAL_EDGES = 1572864
TOTAL_HALO = 131072
N_DOM = 32
N_BAL = 16


def draw_send_edges(key, part):
    key = jax.random.fold_in(key, 11)
    first_key, second_key = jax.random.split(key)
    toward_left = jax.random.randint(first_key, (TOTAL_HALO,), 0, EDGES // 4)
    toward_right = jax.random.randint(second_key, (TOTAL_HALO,), EDGES - EDGES // 4, EDGES)
    toward_left = toward_left.at[0].set(0)
    toward_right = toward_right.at[0].set(EDGES - 1)
    return jnp.stack([toward_left, toward_right]).astype(jnp.int32)


def draw_stencil(key, part):
    key = jax.random.fold_in(key, 12)
    offsets = jax.random.randint(key, (NSTEN, TOTAL_CELLS), -HALO, HALO + 1)
    offsets = offsets.at[0, 0].set(-HALO).at[0, TOTAL_CELLS - 1].set(HALO)
    local_cell = jnp.arange(TOTAL_CELLS, dtype=jnp.int32) % CELLS
    centre = HALO + local_cell * EDGES // CELLS
    return (centre[None, :] + offsets).astype(jnp.int32)


def draw_rain_cols(key, part):
    key = jax.random.fold_in(key, 13)
    many_keys = jax.random.split(key, PARTITIONS)

    def pick_cells(one_key):
        return jax.random.permutation(one_key, CELLS)[:RAIN_MAX]
    lists = jax.vmap(pick_cells)(many_keys)
    return lists.reshape(-1).astype(jnp.int32)


def draw_rain_count(key, part):
    key = jax.random.fold_in(key, 14)
    first_key, second_key, third_key = jax.random.split(key, 3)
    evens = jax.random.randint(first_key, (GROUPS, PAIRS_GROUP), 0, RAIN_MAX + 1)
    chosen = jax.random.randint(second_key, (GROUPS, 1), 0, PAIRS_GROUP)
    flipped = jax.random.randint(third_key, (GROUPS, 1), 0, 2)
    forced = jnp.where(flipped == 0, RAIN_MAX, 0)
    evens = jnp.where(jnp.arange(PAIRS_GROUP, dtype=jnp.int32)[None, :] == chosen, forced, evens)
    return jnp.stack([evens, RAIN_MAX - evens], axis=-1).reshape(-1).astype(jnp.int32)


def steps_of(key, extent, pieces, smallest, top_value):
    def one(position, shards_of):
        heights = jax.random.uniform(jax.random.fold_in(jax.random.fold_in(key, 6), position), (shards_of,), jnp.float32, smallest / len(pieces), top_value / len(pieces))
        return jnp.repeat(jnp.exp(heights), extent[position] // shards_of).reshape((-1,) + (1,) * (len(extent) - position - 1))

    gain = one(*pieces[0])
    for cut in pieces[1:]:
        gain = gain * one(*cut)
    return gain


def normal_values(key, dims, width, bound, cuts=(), kind=jnp.bfloat16):
    result = jax.random.normal(key, dims, jnp.float32) * width
    if len(cuts) > 0:
        result = steps_of(key, dims, cuts, -0.22, 0.18) * result
    return jnp.clip(result, min=-bound, max=bound).astype(kind)


def setup_inputs(seed: int = 0) -> dict:
    streams_of = jax.random.split(jax.random.key(seed), 8)
    return {
        "edge_wind": normal_values(streams_of[0], (LEV, TOTAL_EDGES), 1.0, 6.0, ((1, 512),)),
        "send_edges": draw_send_edges(jax.random.fold_in(streams_of[7], 71), 0),
        "stencil": draw_stencil(jax.random.fold_in(streams_of[7], 71), 0),
        "rbf_coeff": normal_values(streams_of[3], (2, NSTEN, TOTAL_CELLS), NSTEN ** -0.5, 2.0, ((2, 512),), jnp.float32),
        "state": jnp.clip(2.0 * jax.random.uniform(streams_of[4], (4, LEV, TOTAL_CELLS), jnp.float32) ** steps_of(streams_of[4], (4, LEV, TOTAL_CELLS), ((2, 512),), -0.2, 0.2), 0.0, 2.0),
        "rain_cols": draw_rain_cols(jax.random.fold_in(streams_of[7], 71), 0),
        "rain_count": draw_rain_count(jax.random.fold_in(streams_of[7], 71), 0),
    }


def saturate(temper, vapour, cloud_water, rain_water):
    saturation = jnp.exp(0.3 * temper)
    condensed = jnp.maximum((vapour - saturation) / (1.0 + 0.45 * saturation), -cloud_water)
    return (temper + 0.8 * condensed, vapour - condensed, cloud_water + condensed, rain_water)

def rainfall(temper, vapour, cloud_water, rain_water, airspeed):
    levels = temper.shape[0]
    height = jnp.exp(jnp.arange(levels, dtype=jnp.float32) / levels)[:, None]
    falloff = math.exp(-1.0 / levels)
    for substep in range(NSUB):
        saturation = jnp.exp(0.3 * temper)
        collected = 0.5 * jnp.maximum(cloud_water - 0.5, 0.0) + 1.5 * cloud_water * jnp.power(rain_water, 0.875)
        sink_rate = jnp.minimum(collected, cloud_water)
        evaporate = 0.3 * (1.0 + 0.25 * airspeed) * jnp.maximum(saturation - vapour, 0.0) * jnp.power(rain_water, 0.525)
        evaporate = jnp.minimum(evaporate, rain_water)
        temper = temper - 0.8 * evaporate
        vapour = vapour + evaporate
        cloud_water = cloud_water - sink_rate
        middle = rain_water + sink_rate - evaporate
        falling = jnp.minimum(0.5 * jnp.power(middle, 0.1364) * height, 0.9) * middle
        inflow = jnp.concatenate([falling[1:] * falloff, jnp.zeros_like(falling[:1])], axis=0)
        rain_water = middle - falling + inflow
    return (temper, vapour, cloud_water, rain_water)

def reference(edge_wind, send_edges, stencil, rbf_coeff, state, rain_cols, rain_count):
    partitions = N_DOM * N_BAL
    ext_width = EDGES + 2 * HALO
    edge_blocks = edge_wind.reshape(LEV, N_DOM, N_BAL, EDGES)
    send_lists = send_edges.reshape(2, N_DOM, N_BAL, HALO)
    toward_left = jnp.take_along_axis(edge_blocks, jnp.broadcast_to(send_lists[0][None], (LEV, N_DOM, N_BAL, HALO)), axis=3)
    toward_right = jnp.take_along_axis(edge_blocks, jnp.broadcast_to(send_lists[1][None], (LEV, N_DOM, N_BAL, HALO)), axis=3)
    from_left = jnp.roll(toward_right, 1, axis=1)
    from_right = jnp.roll(toward_left, -1, axis=1)
    extended = jnp.concatenate([from_left, edge_blocks, from_right], axis=3).reshape(LEV, partitions * ext_width)
    offsets = jnp.repeat(jnp.arange(partitions, dtype=jnp.int32) * ext_width, CELLS)
    global_index = (stencil + offsets[None, :]).astype(jnp.int32)
    zonal_wind = jnp.zeros((LEV, partitions * CELLS), jnp.float32)
    meridional = jnp.zeros((LEV, partitions * CELLS), jnp.float32)
    for member in range(NSTEN):
        picked = jnp.take(extended, global_index[member], axis=1).astype(jnp.float32)
        zonal_wind = zonal_wind + rbf_coeff[0, member][None, :] * picked
        meridional = meridional + rbf_coeff[1, member][None, :] * picked
    cell_wind = jnp.stack([zonal_wind, meridional]).astype(jnp.bfloat16)
    wind_float = cell_wind.astype(jnp.float32)
    airspeed = jnp.sqrt(wind_float[0] * wind_float[0] + wind_float[1] * wind_float[1] + 1.0)
    adjusted = saturate(state[0], state[1], state[2], state[3])
    cell_base = (jnp.arange(partitions, dtype=jnp.int32) * CELLS)[:, None]
    global_cols = (rain_cols.reshape(partitions, RAIN_MAX) + cell_base).reshape(-1).astype(jnp.int32)
    live_mask = (jnp.arange(RAIN_MAX, dtype=jnp.int32)[None, :] < rain_count[:, None]).reshape(-1)
    current = tuple((jnp.take(field_now, global_cols, axis=1) for field_now in adjusted))
    speed_cols = jnp.take(airspeed, global_cols, axis=1)
    rained = rainfall(current[0], current[1], current[2], current[3], speed_cols)
    updated = jnp.stack([field_now.at[:, global_cols].set(jnp.where(live_mask[None, :], after, before)) for field_now, after, before in zip(adjusted, rained, current)])
    return (cell_wind, updated - state)
```

```python
import math

import jax
import jax.numpy as jnp
from jax import lax
from jax.experimental import pallas as pl
from jax.experimental.pallas import tpu as pltpu
from jax.sharding import PartitionSpec as P

NSUB = 3
LOG2E = math.log2(math.e)
LANES = 128
ROWS = 16
PIECES = 4
VMEM_BYTES = 40 * 1024 * 1024
RING = 8


def pick_sends(send_ref, edge_ref, arrivals, left_ref, right_ref, stack_ref, found_ref):
    edges = edge_ref.shape[1]
    width = send_ref.shape[1]
    chunk = 256
    span = edges // len(arrivals)
    wanted = jnp.concatenate([send_ref[0:1, :], send_ref[1:2, :]], axis=1)
    low = jnp.broadcast_to(lax.rem(wanted, chunk), (ROWS, 2 * width)).astype(jnp.int16)
    high = jnp.broadcast_to(wanted // chunk, (8, 2 * width))
    rows = lax.broadcasted_iota(jnp.int32, (ROWS, 2 * width), 0)
    picker = jnp.concatenate(
        [
            jnp.where(low == (rows + row).astype(jnp.int16), jnp.bfloat16(1), jnp.bfloat16(0))
            for row in range(0, chunk, ROWS)
        ],
        axis=0,
    )
    levels = edge_ref.shape[0]
    step = stack_ref.shape[0] // (edges // chunk)
    for first in range(0, edges, chunk):
        if first % span == 0:
            arrivals[first // span].wait()
        base = first // chunk * step
        stack_ref[base : base + levels, :] = edge_ref[:, first : first + chunk]
    for side, out_ref in ((0, left_ref), (1, right_ref)):
        columns = slice(side * width, (side + 1) * width)
        found_ref[...] = jnp.dot(
            stack_ref[...], picker[:, columns], preferred_element_type=jnp.float32
        )
        here = [high[:, columns] == n for n in range(edges // chunk)]
        total = []
        for base in range(0, levels, 8):
            some = found_ref[base : base + 8, :]
            for n in range(1, edges // chunk):
                some = jnp.where(here[n], found_ref[n * step + base : n * step + base + 8, :], some)
            total.append(some)
        out_ref[...] = jnp.concatenate(total, axis=0)[:levels].astype(jnp.bfloat16)


def listed_mask(cols_ref, count):
    slots = cols_ref.shape[1]
    cols = cols_ref[...]
    live = lax.broadcasted_iota(jnp.int32, (1, slots), 1) < count
    high = jnp.where(live, cols // LANES, -1)
    low = lax.rem(cols, LANES)
    rows = jnp.where(lax.broadcasted_iota(jnp.int32, (8, slots), 0) == high, 1.0, 0.0)
    lanes = jnp.where(lax.broadcasted_iota(jnp.int32, (LANES, slots), 0) == low, 1.0, 0.0)
    return lax.dot_general(
        rows.astype(jnp.bfloat16),
        lanes.astype(jnp.bfloat16),
        (((1,), (1,)), ((), ())),
        preferred_element_type=jnp.float32,
    )


def merge_members(sten_ref, rbf_ref, pos_ref, zon_ref, mer_ref, tmp_ref, fold):
    members = sten_ref.shape[0]
    blocks = sten_ref.shape[1] // LANES
    for k in range(blocks):
        tmp_ref[ROWS * k : ROWS * k + members, :] = (
            sten_ref[:, LANES * k : LANES * (k + 1)] - 3 * LANES * k
        )
    places, zonal, merid = [], [], []
    for s in range(members):
        places.append(tmp_ref[pl.ds(s, blocks, stride=ROWS), :])
        zonal.append(rbf_ref[pl.ds(2 * blocks * s, blocks, stride=2), :])
        merid.append(rbf_ref[pl.ds(2 * blocks * s + 1, blocks, stride=2), :])
    for t in range(members):
        z, m = zonal[t], merid[t]
        for s in range(t):
            same = places[s] == places[t]
            z = z + jnp.where(same, zonal[s], 0.0)
            m = m + jnp.where(same, merid[s], 0.0)
        rows = slice(blocks * t, blocks * (t + 1))
        pos_ref[rows, :] = jnp.where(places[t] >= fold, places[t] - fold, places[t])
        zon_ref[rows, :] = z
        mer_ref[rows, :] = m


def build_table(k, members, blocks, fold, window, pos_ref, zon_ref, mer_ref, table_ref):
    def spread(ref, s, kind):
        row = ref[pl.ds(blocks * s + k, 1), :]
        return jnp.broadcast_to(row, (ROWS, LANES)).astype(kind)

    places = [spread(pos_ref, s, jnp.int16) for s in range(members)]
    zonal = [spread(zon_ref, s, jnp.bfloat16) for s in range(members)]
    merid = [spread(mer_ref, s, jnp.bfloat16) for s in range(members)]
    rows = lax.broadcasted_iota(jnp.int32, (ROWS, LANES), 0)
    first = (3 * lax.broadcasted_iota(jnp.int32, (ROWS, LANES), 1)).astype(jnp.int16)
    none = jnp.zeros((ROWS, LANES), jnp.bfloat16)
    for row in range(0, fold, ROWS):
        here = (rows + row).astype(jnp.int16)
        z, m = none, none
        for s in range(members):
            hit = places[s] == here
            z = jnp.where(hit, zonal[s], z)
            m = jnp.where(hit, merid[s], m)
        if row + fold < window:
            low = first <= here
            table_ref[row : row + ROWS, :LANES] = jnp.where(low, z, none)
            table_ref[row : row + ROWS, LANES:] = jnp.where(low, m, none)
            table_ref[fold + row : fold + row + ROWS, :LANES] = jnp.where(low, none, z)
            table_ref[fold + row : fold + row + ROWS, LANES:] = jnp.where(low, none, m)
        else:
            table_ref[row : row + ROWS, :LANES] = z
            table_ref[row : row + ROWS, LANES:] = m


def keep_wind(k, levels, blocks, wind, wide_ref):
    for base in range(0, levels, 8):
        count = min(8, levels - base)
        for c in range(2):
            wide_ref[pl.ds(2 * (blocks * base + k) + c, count, stride=2 * blocks), :] = wind[
                base : base + count, LANES * c : LANES * (c + 1)
            ]


def rain_column(k, levels, blocks, listed, wind, state_ref, tend_ref, dry_ref):
    if listed is not None:
        listed = jnp.broadcast_to(listed, (8, LANES)) > 0.5
    falloff = math.exp(-1.0 / levels)
    stride = 4 * blocks
    above = [None] * NSUB
    for base in reversed(range(0, levels, 8)):
        count = min(8, levels - base)
        u = wind[base : base + count, :LANES]
        v = wind[base : base + count, LANES:]
        airspeed = jnp.sqrt(u * u + v * v + 1.0)
        factor = 0.3 + 0.075 * airspeed
        before = [
            state_ref[pl.ds(stride * base + 4 * k + f, count, stride=stride), :] for f in range(4)
        ]
        t, qv, qc, qr = before
        qvs = jnp.exp2((0.3 * LOG2E) * t)
        cond = jnp.maximum((qv - qvs) / (1.0 + 0.45 * qvs), -qc)
        t, qv, qc = t + 0.8 * cond, qv - cond, qc + cond
        adjusted = (t, qv, qc, qr)
        level = (lax.broadcasted_iota(jnp.int32, (count, LANES), 0) + base).astype(jnp.float32)
        height = level * (LOG2E / levels) - 1.0
        for substep in range(NSUB):
            qvs = jnp.exp2((0.3 * LOG2E) * t)
            log_rain = jnp.log2(qr)
            collected = 0.5 * jnp.maximum(qc - 0.5, 0.0) + 1.5 * qc * jnp.exp2(0.875 * log_rain)
            sink = jnp.minimum(collected, qc)
            evap = factor * jnp.maximum(qvs - qv, 0.0) * jnp.exp2(0.525 * log_rain)
            evap = jnp.minimum(evap, qr)
            t = t - 0.8 * evap
            qv = qv + evap
            qc = qc - sink
            mid = (qr + sink) - evap
            fall = jnp.minimum(jnp.exp2(0.1364 * jnp.log2(mid) + height), 0.9) * mid
            top = above[substep]
            if top is None:
                top = jnp.zeros((1, LANES), jnp.float32)
            inflow = jnp.concatenate([fall[1:], top], axis=0)
            above[substep] = fall[:1]
            qr = (mid - fall) + falloff * inflow
        rained = (t, qv, qc, qr)
        for f in range(4):
            rows = pl.ds(stride * base + 4 * k + f, count, stride=stride)
            if listed is None:
                tend_ref[rows, :] = rained[f] - before[f]
                dry_ref[rows, :] = adjusted[f] - before[f]
            else:
                after = jnp.where(listed[:count], rained[f], adjusted[f])
                tend_ref[rows, :] = after - before[f]


def inner_cells(
    edge_ref,
    sten_ref,
    rbf_ref,
    state_ref,
    tend_ref,
    dry_ref,
    wide_ref,
    part_ref,
    edge_table_ref,
    pos_ref,
    zon_ref,
    mer_ref,
    tmp_ref,
    table_ref,
):
    levels, edges = edge_ref.shape
    members, cells = sten_ref.shape
    blocks = cells // LANES
    halo = edge_table_ref.shape[1]
    window = table_ref.shape[0]
    fold = 2 * halo + ROWS
    tend_rows = tend_ref.reshape(tend_ref.shape[0] * 4 * blocks, LANES)
    dry_rows = dry_ref.reshape(dry_ref.shape[0] * 4 * blocks, LANES)
    merge_members(sten_ref, rbf_ref, pos_ref, zon_ref, mer_ref, tmp_ref, fold)

    def table(k):
        build_table(k, members, blocks, fold, window, pos_ref, zon_ref, mer_ref, table_ref)

    def inside(k, carry):
        table(k)
        start = pl.multiple_of(3 * LANES * k - halo, LANES)
        wind = jnp.dot(
            edge_ref[:, pl.ds(start, window)], table_ref[...], preferred_element_type=jnp.float32
        )
        keep_wind(k, levels, blocks, wind, wide_ref)
        rain_column(k, levels, blocks, None, wind, state_ref, tend_rows, dry_rows)
        return carry

    lax.fori_loop(1, blocks - 1, inside, 0)

    def border(side, carry):
        table(side * (blocks - 1))
        keep = pl.multiple_of(side * (window - halo), LANES)
        rest = pl.multiple_of((1 - side) * halo, LANES)
        start = pl.multiple_of(side * (edges - window + halo), LANES)
        edge_table_ref[side] = table_ref[pl.ds(keep, halo), :]
        part_ref[side] = jnp.dot(
            edge_ref[:, pl.ds(start, window - halo)],
            table_ref[pl.ds(rest, window - halo), :],
            preferred_element_type=jnp.float32,
        )
        return carry

    lax.fori_loop(0, 2, border, 0)


def is_early():
    dom, bal = lax.axis_index("dom"), lax.axis_index("bal")
    return jnp.logical_and(lax.rem(dom, RING) == 0, dom + bal > 0)


def first_kernel(*refs):
    sources, refs = refs[:6], refs[6:]
    left_ref, right_ref = refs[:2]
    held, results, refs = refs[2:7], refs[7:12], refs[12:]
    send_ref, work, sem = refs[0], refs[3:8], refs[8]
    edge_in, rest_in = sources[1], sources[2:]
    edge_ref = held[0]
    edges = edge_ref.shape[1]
    span = edges // PIECES
    first = pltpu.make_async_copy(sources[0], send_ref, sem.at[0])
    first.start()
    arrivals = []
    for piece in range(PIECES):
        part = pl.ds(piece * span, span)
        arrivals.append(
            pltpu.make_async_copy(edge_in.at[:, part], edge_ref.at[:, part], sem.at[1 + piece])
        )
        arrivals[-1].start()
    others = []
    for n, (source, target) in enumerate(zip(rest_in, held[1:])):
        part = pl.ds(0, source.shape[0])
        others.append(pltpu.make_async_copy(source, target.at[part], sem.at[1 + PIECES + n]))
        others[-1].start()
    first.wait()
    pick_sends(send_ref, edge_ref, arrivals, left_ref, right_ref, *refs[1:3])
    for copy in others:
        copy.wait()

    @pl.when(is_early())
    def _():
        inner_cells(*held[:4], *results, *work)


def second_kernel(*refs):
    held, count_ref, left_ref, refs = refs[:5], refs[5], refs[6], refs[12:]
    results, mask_ref, work = refs[:5], refs[5], refs[6:]
    tend_ref, dry_ref, wide_ref, part_ref, edge_table_ref = results
    levels = left_ref.shape[0]
    blocks = mask_ref.shape[0]

    @pl.when(jnp.logical_not(is_early()))
    def _():
        inner_cells(*held[:4], *results, *work)

    mask = listed_mask(held[4], count_ref[0])
    mask_ref[...] = mask
    group = 8
    fields = group // 2
    listed = [
        jnp.concatenate(
            [
                jnp.broadcast_to(mask[k : k + 1], (fields, LANES)),
                jnp.broadcast_to(mask[k + 1 : k + 2], (fields, LANES)),
            ],
            axis=0,
        )
        > 0.5
        for k in range(0, blocks, 2)
    ]

    def choose(level, carry):
        for n, here in enumerate(listed):
            rows = slice(group * n, group * (n + 1))
            tend_ref[level, rows] = jnp.where(here, tend_ref[level, rows], dry_ref[level, rows])
        return carry

    lax.fori_loop(0, levels, choose, 0, unroll=5)
    wind = part_ref[0] + jnp.dot(
        left_ref[...], edge_table_ref[0], preferred_element_type=jnp.float32
    )
    tend_rows = tend_ref.reshape(tend_ref.shape[0] * 4 * blocks, LANES)
    keep_wind(0, levels, blocks, wind, wide_ref)
    rain_column(0, levels, blocks, mask[:1], wind, held[3], tend_rows, None)


def outer_kernel(
    right_ref,
    part_ref,
    edge_table_ref,
    mask_ref,
    state_ref,
    tend_in,
    wide_in,
    tend_out,
    wind_out,
    tend_ref,
    wide_ref,
    wind_ref,
    sem,
):
    del tend_in, wide_in
    levels = right_ref.shape[0]
    blocks = mask_ref.shape[0]
    group = 8
    last = blocks - 1

    def send(first, count, n):
        part = pl.ds(first, count)
        copy = pltpu.make_async_copy(
            tend_ref.at[pl.ds(0, levels), part], tend_out.at[:, part], sem.at[n]
        )
        copy.start()
        return copy

    copies = [send(0, 4 * blocks - group, 0)]
    wind = part_ref[1] + jnp.dot(
        right_ref[...], edge_table_ref[1], preferred_element_type=jnp.float32
    )
    keep_wind(last, levels, blocks, wind, wide_ref)
    for level in range(levels):
        rows = slice(2 * blocks * level, 2 * blocks * (level + 1))
        wind_ref[rows, :] = wide_ref[rows, :].astype(jnp.bfloat16)
    copies.append(pltpu.make_async_copy(wind_ref, wind_out, sem.at[1]))
    copies[-1].start()
    tend_rows = tend_ref.reshape(tend_ref.shape[0] * 4 * blocks, LANES)
    rain_column(last, levels, blocks, mask_ref[last:blocks, :], wind, state_ref, tend_rows, None)
    copies.append(send(4 * blocks - group, group, 2))
    for copy in copies:
        copy.wait()


def local(edge_wind, send_edges, stencil, rbf_coeff, state, rain_cols, rain_count):
    levels, edges = edge_wind.shape
    halo = send_edges.shape[1]
    members, cells = stencil.shape
    blocks = cells // LANES
    slots = rain_cols.shape[0]
    padded = -(-levels // 8) * 8
    window = 3 * LANES + 2 * halo
    vmem = pl.BlockSpec(memory_space=pltpu.VMEM)
    anywhere = pl.BlockSpec(memory_space=pltpu.HBM)
    f32, bf16, i32 = jnp.float32, jnp.bfloat16, jnp.int32
    shape = jax.ShapeDtypeStruct
    state_rows = jnp.transpose(state.reshape(4, levels, blocks, LANES), (1, 2, 0, 3)).reshape(
        levels * blocks * 4, LANES
    )
    rbf_rows = jnp.transpose(rbf_coeff.reshape(2, members, blocks, LANES), (1, 2, 0, 3)).reshape(
        members * blocks * 2, LANES
    )
    held_shapes = [
        shape((levels, edges), bf16),
        shape((members, cells), i32),
        shape((members * blocks * 2, LANES), f32),
        shape((padded * blocks * 4, LANES), f32),
        shape((1, slots), i32),
    ]
    result_shapes = [
        shape((padded, blocks * 4, LANES), f32),
        shape((padded, blocks * 4, LANES), f32),
        shape((padded * blocks * 2, LANES), f32),
        shape((2, levels, 2 * LANES), f32),
        shape((2, halo, 2 * LANES), bf16),
    ]
    work = [
        pltpu.VMEM((members * blocks, LANES), i32),
        pltpu.VMEM((members * blocks, LANES), f32),
        pltpu.VMEM((members * blocks, LANES), f32),
        pltpu.VMEM((ROWS * blocks, LANES), i32),
        pltpu.VMEM((window, 2 * LANES), bf16),
    ]
    params = pltpu.CompilerParams(vmem_limit_bytes=VMEM_BYTES)
    first = pl.pallas_call(
        first_kernel,
        out_shape=[shape((levels, halo), bf16)] * 2 + held_shapes + result_shapes,
        in_specs=[anywhere] * 6,
        out_specs=[vmem] * 12,
        scratch_shapes=[
            pltpu.VMEM((2, halo), i32),
            pltpu.VMEM((edges // 256 * 64, 256), bf16),
            pltpu.VMEM((edges // 256 * 64, halo), f32),
        ]
        + work
        + [pltpu.SemaphoreType.DMA((1 + PIECES + 4,))],
        compiler_params=params,
        name="first_cells",
    )(
        *[
            pltpu.with_memory_space_constraint(array, pltpu.HBM)
            for array in (
                send_edges,
                edge_wind,
                stencil,
                rbf_rows,
                state_rows,
                rain_cols.reshape(1, slots),
            )
        ],
    )
    toward_left, toward_right = first[:2]
    held, results = first[2:7], first[7:]
    count = lax.axis_size("dom")
    from_left = lax.ppermute(toward_right, "dom", [(i, (i + 1) % count) for i in range(count)])
    from_right = lax.ppermute(toward_left, "dom", [((i + 1) % count, i) for i in range(count)])
    tend, _, wide, part, edge_table, mask = pl.pallas_call(
        second_kernel,
        out_shape=result_shapes + [shape((blocks, LANES), f32)],
        in_specs=[vmem] * 5 + [pl.BlockSpec(memory_space=pltpu.SMEM)] + [vmem] * 6,
        out_specs=[vmem] * 6,
        scratch_shapes=work,
        input_output_aliases={7 + n: n for n in range(5)},
        compiler_params=params,
        name="second_cells",
    )(*held, rain_count, from_left, *results)
    tend, wind, _, _ = pl.pallas_call(
        outer_kernel,
        out_shape=[
            shape((levels, blocks * 4, LANES), f32),
            shape((levels * blocks * 2, LANES), bf16),
            result_shapes[0],
            result_shapes[2],
        ],
        in_specs=[vmem] * 7,
        out_specs=[anywhere] * 2 + [vmem] * 2,
        scratch_shapes=[
            pltpu.VMEM((levels * blocks * 2, LANES), bf16),
            pltpu.SemaphoreType.DMA((3,)),
        ],
        input_output_aliases={5: 2, 6: 3},
        compiler_params=params,
        name="outer_cells",
    )(from_right, part, edge_table, mask, held[3], tend, wide)
    tendency = jnp.transpose(tend.reshape(levels, blocks, 4, LANES), (2, 0, 1, 3)).reshape(
        4, levels, cells
    )
    cell_wind = jnp.transpose(wind.reshape(levels, blocks, 2, LANES), (2, 0, 1, 3)).reshape(
        2, levels, cells
    )
    return (cell_wind, tendency)


def solution(mesh):
    placed = (
        P(None, ("dom", "bal")),
        P(None, ("dom", "bal")),
        P(None, ("dom", "bal")),
        P(None, None, ("dom", "bal")),
        P(None, None, ("dom", "bal")),
        P(("dom", "bal")),
        P(("dom", "bal")),
    )
    return jax.shard_map(
        local,
        mesh=mesh,
        in_specs=placed,
        out_specs=(P(None, None, ("dom", "bal")), P(None, None, ("dom", "bal"))),
        check_vma=False,
    )
```

```python
import math

import jax
import jax.numpy as jnp
from jax import lax
from jax.experimental import pallas as pl
from jax.experimental.pallas import tpu as pltpu
from jax.sharding import PartitionSpec as P

NSUB = 3
LOG2E = math.log2(math.e)
LANES = 128
ROWS = 16
PIECES = 1
VMEM_BYTES = 40 * 1024 * 1024
RING = 8


def pick_sends(send_ref, edge_ref, arrivals, left_ref, right_ref, stack_ref, found_ref):
    edges = edge_ref.shape[1]
    width = send_ref.shape[1]
    chunk = 256
    span = edges // len(arrivals)
    wanted = jnp.concatenate([send_ref[0:1, :], send_ref[1:2, :]], axis=1)
    low = jnp.broadcast_to(lax.rem(wanted, chunk), (ROWS, 2 * width)).astype(jnp.int16)
    high = jnp.broadcast_to(wanted // chunk, (8, 2 * width))
    rows = lax.broadcasted_iota(jnp.int32, (ROWS, 2 * width), 0)
    picker = jnp.concatenate(
        [
            jnp.where(low == (rows + row).astype(jnp.int16), jnp.bfloat16(1), jnp.bfloat16(0))
            for row in range(0, chunk, ROWS)
        ],
        axis=0,
    )
    levels = edge_ref.shape[0]
    step = stack_ref.shape[0] // (edges // chunk)
    for first in range(0, edges, chunk):
        if first % span == 0:
            arrivals[first // span].wait()
        base = first // chunk * step
        stack_ref[base : base + levels, :] = edge_ref[:, first : first + chunk]
    found_ref[...] = jnp.dot(stack_ref[...], picker, preferred_element_type=jnp.float32)
    here = [high == n for n in range(edges // chunk)]
    total = []
    for base in range(0, levels, 8):
        some = found_ref[base : base + 8, :]
        for n in range(1, edges // chunk):
            some = jnp.where(here[n], found_ref[n * step + base : n * step + base + 8, :], some)
        total.append(some)
    total = jnp.concatenate(total, axis=0)[:levels].astype(jnp.bfloat16)
    left_ref[...] = total[:, :width]
    right_ref[...] = total[:, width:]


def listed_mask(cols_ref, count):
    slots = cols_ref.shape[1]
    cols = cols_ref[...]
    live = lax.broadcasted_iota(jnp.int32, (1, slots), 1) < count
    high = jnp.where(live, cols // LANES, -1)
    low = lax.rem(cols, LANES)
    rows = jnp.where(lax.broadcasted_iota(jnp.int32, (8, slots), 0) == high, 1.0, 0.0)
    lanes = jnp.where(lax.broadcasted_iota(jnp.int32, (LANES, slots), 0) == low, 1.0, 0.0)
    return lax.dot_general(
        rows.astype(jnp.bfloat16),
        lanes.astype(jnp.bfloat16),
        (((1,), (1,)), ((), ())),
        preferred_element_type=jnp.float32,
    )


def merge_members(sten_ref, rbf_ref, pos_ref, zon_ref, mer_ref, tmp_ref, fold):
    members = sten_ref.shape[0]
    blocks = sten_ref.shape[1] // LANES
    for k in range(blocks):
        tmp_ref[ROWS * k : ROWS * k + members, :] = (
            sten_ref[:, LANES * k : LANES * (k + 1)] - 3 * LANES * k
        )
    places, zonal, merid = [], [], []
    for s in range(members):
        places.append(tmp_ref[pl.ds(s, blocks, stride=ROWS), :])
        zonal.append(rbf_ref[pl.ds(2 * blocks * s, blocks, stride=2), :])
        merid.append(rbf_ref[pl.ds(2 * blocks * s + 1, blocks, stride=2), :])
    for t in range(members):
        z, m = zonal[t], merid[t]
        for s in range(t):
            same = places[s] == places[t]
            z = z + jnp.where(same, zonal[s], 0.0)
            m = m + jnp.where(same, merid[s], 0.0)
        rows = slice(blocks * t, blocks * (t + 1))
        pos_ref[rows, :] = jnp.where(places[t] >= fold, places[t] - fold, places[t])
        zon_ref[rows, :] = z
        mer_ref[rows, :] = m


def build_table(k, members, blocks, fold, window, pos_ref, zon_ref, mer_ref, table_ref):
    def spread(ref, s, kind):
        row = ref[pl.ds(blocks * s + k, 1), :]
        return jnp.broadcast_to(row, (ROWS, LANES)).astype(kind)

    places = [spread(pos_ref, s, jnp.int16) for s in range(members)]
    zonal = [spread(zon_ref, s, jnp.bfloat16) for s in range(members)]
    merid = [spread(mer_ref, s, jnp.bfloat16) for s in range(members)]
    rows = lax.broadcasted_iota(jnp.int32, (ROWS, LANES), 0)
    first = (3 * lax.broadcasted_iota(jnp.int32, (ROWS, LANES), 1)).astype(jnp.int16)
    none = jnp.zeros((ROWS, LANES), jnp.bfloat16)
    for row in range(0, fold, ROWS):
        here = (rows + row).astype(jnp.int16)
        z, m = none, none
        for s in range(members):
            hit = places[s] == here
            z = jnp.where(hit, zonal[s], z)
            m = jnp.where(hit, merid[s], m)
        if row + fold < window:
            low = first <= here
            table_ref[row : row + ROWS, :LANES] = jnp.where(low, z, none)
            table_ref[row : row + ROWS, LANES:] = jnp.where(low, m, none)
            table_ref[fold + row : fold + row + ROWS, :LANES] = jnp.where(low, none, z)
            table_ref[fold + row : fold + row + ROWS, LANES:] = jnp.where(low, none, m)
        else:
            table_ref[row : row + ROWS, :LANES] = z
            table_ref[row : row + ROWS, LANES:] = m


def keep_wind(k, levels, blocks, wind, wide_ref):
    for base in range(0, levels, 8):
        count = min(8, levels - base)
        for c in range(2):
            wide_ref[pl.ds(2 * (blocks * base + k) + c, count, stride=2 * blocks), :] = wind[
                base : base + count, LANES * c : LANES * (c + 1)
            ]


def rain_column(k, levels, blocks, listed, wind, state_ref, tend_ref, dry_ref):
    if listed is not None:
        listed = jnp.broadcast_to(listed, (8, LANES)) > 0.5
    falloff = math.exp(-1.0 / levels)
    stride = 4 * blocks
    above = [None] * NSUB
    for base in reversed(range(0, levels, 8)):
        count = min(8, levels - base)
        u = wind[base : base + count, :LANES]
        v = wind[base : base + count, LANES:]
        airspeed = jnp.sqrt(u * u + v * v + 1.0)
        factor = 0.3 + 0.075 * airspeed
        before = [
            state_ref[pl.ds(stride * base + 4 * k + f, count, stride=stride), :] for f in range(4)
        ]
        t, qv, qc, qr = before
        qvs = jnp.exp2((0.3 * LOG2E) * t)
        cond = jnp.maximum((qv - qvs) / (1.0 + 0.45 * qvs), -qc)
        t, qv, qc = t + 0.8 * cond, qv - cond, qc + cond
        adjusted = (t, qv, qc, qr)
        level = (lax.broadcasted_iota(jnp.int32, (count, LANES), 0) + base).astype(jnp.float32)
        height = level * (LOG2E / levels) - 1.0
        for substep in range(NSUB):
            qvs = jnp.exp2((0.3 * LOG2E) * t)
            log_rain = jnp.log2(qr)
            collected = 0.5 * jnp.maximum(qc - 0.5, 0.0) + 1.5 * qc * jnp.exp2(0.875 * log_rain)
            sink = jnp.minimum(collected, qc)
            evap = factor * jnp.maximum(qvs - qv, 0.0) * jnp.exp2(0.525 * log_rain)
            evap = jnp.minimum(evap, qr)
            t = t - 0.8 * evap
            qv = qv + evap
            qc = qc - sink
            mid = (qr + sink) - evap
            fall = jnp.minimum(jnp.exp2(0.1364 * jnp.log2(mid) + height), 0.9) * mid
            top = above[substep]
            if top is None:
                top = jnp.zeros((1, LANES), jnp.float32)
            inflow = jnp.concatenate([fall[1:], top], axis=0)
            above[substep] = fall[:1]
            qr = (mid - fall) + falloff * inflow
        rained = (t, qv, qc, qr)
        for f in range(4):
            rows = pl.ds(stride * base + 4 * k + f, count, stride=stride)
            if listed is None:
                tend_ref[rows, :] = rained[f] - before[f]
                dry_ref[rows, :] = adjusted[f] - before[f]
            else:
                after = jnp.where(listed[:count], rained[f], adjusted[f])
                tend_ref[rows, :] = after - before[f]


def inner_cells(
    edge_ref,
    sten_ref,
    rbf_ref,
    state_ref,
    tend_ref,
    dry_ref,
    wide_ref,
    part_ref,
    edge_table_ref,
    pos_ref,
    zon_ref,
    mer_ref,
    tmp_ref,
    table_ref,
):
    levels, edges = edge_ref.shape
    members, cells = sten_ref.shape
    blocks = cells // LANES
    halo = edge_table_ref.shape[1]
    window = table_ref.shape[0]
    fold = 2 * halo + ROWS
    tend_rows = tend_ref.reshape(tend_ref.shape[0] * 4 * blocks, LANES)
    dry_rows = dry_ref.reshape(dry_ref.shape[0] * 4 * blocks, LANES)
    merge_members(sten_ref, rbf_ref, pos_ref, zon_ref, mer_ref, tmp_ref, fold)

    def table(k):
        build_table(k, members, blocks, fold, window, pos_ref, zon_ref, mer_ref, table_ref)

    def inside(k, carry):
        table(k)
        start = pl.multiple_of(3 * LANES * k - halo, LANES)
        wind = jnp.dot(
            edge_ref[:, pl.ds(start, window)], table_ref[...], preferred_element_type=jnp.float32
        )
        keep_wind(k, levels, blocks, wind, wide_ref)
        rain_column(k, levels, blocks, None, wind, state_ref, tend_rows, dry_rows)
        return carry

    lax.fori_loop(1, blocks - 1, inside, 0)

    def border(side, carry):
        table(side * (blocks - 1))
        keep = pl.multiple_of(side * (window - halo), LANES)
        rest = pl.multiple_of((1 - side) * halo, LANES)
        start = pl.multiple_of(side * (edges - window + halo), LANES)
        edge_table_ref[side] = table_ref[pl.ds(keep, halo), :]
        part_ref[side] = jnp.dot(
            edge_ref[:, pl.ds(start, window - halo)],
            table_ref[pl.ds(rest, window - halo), :],
            preferred_element_type=jnp.float32,
        )
        return carry

    lax.fori_loop(0, 2, border, 0)


def is_early():
    dom, bal = lax.axis_index("dom"), lax.axis_index("bal")
    return jnp.logical_and(lax.rem(dom, RING) == 0, dom + bal > 0)


def first_kernel(*refs):
    sources, refs = refs[:6], refs[6:]
    left_ref, right_ref = refs[:2]
    held, results, refs = refs[2:7], refs[7:12], refs[12:]
    send_ref, work, sem = refs[0], refs[3:8], refs[8]
    edge_in, rest_in = sources[1], sources[2:]
    edge_ref = held[0]
    edges = edge_ref.shape[1]
    span = edges // PIECES
    arrivals = []
    for piece in range(PIECES):
        part = pl.ds(piece * span, span)
        arrivals.append(
            pltpu.make_async_copy(edge_in.at[:, part], edge_ref.at[:, part], sem.at[1 + piece])
        )
        arrivals[-1].start()
    first = pltpu.make_async_copy(sources[0], send_ref, sem.at[0])
    first.start()
    others = []
    for n, (source, target) in enumerate(zip(rest_in, held[1:])):
        part = pl.ds(0, source.shape[0])
        others.append(pltpu.make_async_copy(source, target.at[part], sem.at[1 + PIECES + n]))
        others[-1].start()
    first.wait()
    pick_sends(send_ref, edge_ref, arrivals, left_ref, right_ref, *refs[1:3])
    for copy in others:
        copy.wait()

    @pl.when(is_early())
    def _():
        inner_cells(*held[:4], *results, *work)


def second_kernel(*refs):
    held, count_ref, left_ref, refs = refs[:5], refs[5], refs[6], refs[12:]
    results, mask_ref, work = refs[:5], refs[5], refs[6:]
    tend_ref, dry_ref, wide_ref, part_ref, edge_table_ref = results
    levels = left_ref.shape[0]
    blocks = mask_ref.shape[0]

    @pl.when(jnp.logical_not(is_early()))
    def _():
        inner_cells(*held[:4], *results, *work)

    mask = listed_mask(held[4], count_ref[0])
    mask_ref[...] = mask
    group = 8
    fields = group // 2
    listed = [
        jnp.concatenate(
            [
                jnp.broadcast_to(mask[k : k + 1], (fields, LANES)),
                jnp.broadcast_to(mask[k + 1 : k + 2], (fields, LANES)),
            ],
            axis=0,
        )
        > 0.5
        for k in range(0, blocks, 2)
    ]

    def choose(level, carry):
        for n, here in enumerate(listed):
            rows = slice(group * n, group * (n + 1))
            tend_ref[level, rows] = jnp.where(here, tend_ref[level, rows], dry_ref[level, rows])
        return carry

    lax.fori_loop(0, levels, choose, 0, unroll=5)
    wind = part_ref[0] + jnp.dot(
        left_ref[...], edge_table_ref[0], preferred_element_type=jnp.float32
    )
    tend_rows = tend_ref.reshape(tend_ref.shape[0] * 4 * blocks, LANES)
    keep_wind(0, levels, blocks, wind, wide_ref)
    rain_column(0, levels, blocks, mask[:1], wind, held[3], tend_rows, None)


def outer_kernel(
    right_ref,
    part_ref,
    edge_table_ref,
    mask_ref,
    state_ref,
    tend_in,
    wide_in,
    tend_out,
    wind_out,
    tend_ref,
    wide_ref,
    wind_ref,
    sem,
):
    del tend_in, wide_in
    levels = right_ref.shape[0]
    blocks = mask_ref.shape[0]
    group = 8
    last = blocks - 1

    def send(first, count, n):
        part = pl.ds(first, count)
        copy = pltpu.make_async_copy(
            tend_ref.at[pl.ds(0, levels), part], tend_out.at[:, part], sem.at[n]
        )
        copy.start()
        return copy

    copies = [send(0, 4 * blocks - group, 0)]
    wind = part_ref[1] + jnp.dot(
        right_ref[...], edge_table_ref[1], preferred_element_type=jnp.float32
    )
    keep_wind(last, levels, blocks, wind, wide_ref)
    for level in range(levels):
        rows = slice(2 * blocks * level, 2 * blocks * (level + 1))
        wind_ref[rows, :] = wide_ref[rows, :].astype(jnp.bfloat16)
    copies.append(pltpu.make_async_copy(wind_ref, wind_out, sem.at[1]))
    copies[-1].start()
    tend_rows = tend_ref.reshape(tend_ref.shape[0] * 4 * blocks, LANES)
    rain_column(last, levels, blocks, mask_ref[last:blocks, :], wind, state_ref, tend_rows, None)
    copies.append(send(4 * blocks - group, group, 2))
    for copy in copies:
        copy.wait()


def local(edge_wind, send_edges, stencil, rbf_coeff, state, rain_cols, rain_count):
    levels, edges = edge_wind.shape
    halo = send_edges.shape[1]
    members, cells = stencil.shape
    blocks = cells // LANES
    slots = rain_cols.shape[0]
    padded = -(-levels // 8) * 8
    window = 3 * LANES + 2 * halo
    vmem = pl.BlockSpec(memory_space=pltpu.VMEM)
    anywhere = pl.BlockSpec(memory_space=pltpu.HBM)
    f32, bf16, i32 = jnp.float32, jnp.bfloat16, jnp.int32
    shape = jax.ShapeDtypeStruct
    state_rows = jnp.transpose(state.reshape(4, levels, blocks, LANES), (1, 2, 0, 3)).reshape(
        levels * blocks * 4, LANES
    )
    rbf_rows = jnp.transpose(rbf_coeff.reshape(2, members, blocks, LANES), (1, 2, 0, 3)).reshape(
        members * blocks * 2, LANES
    )
    held_shapes = [
        shape((levels, edges), bf16),
        shape((members, cells), i32),
        shape((members * blocks * 2, LANES), f32),
        shape((padded * blocks * 4, LANES), f32),
        shape((1, slots), i32),
    ]
    result_shapes = [
        shape((padded, blocks * 4, LANES), f32),
        shape((padded, blocks * 4, LANES), f32),
        shape((padded * blocks * 2, LANES), f32),
        shape((2, levels, 2 * LANES), f32),
        shape((2, halo, 2 * LANES), bf16),
    ]
    work = [
        pltpu.VMEM((members * blocks, LANES), i32),
        pltpu.VMEM((members * blocks, LANES), f32),
        pltpu.VMEM((members * blocks, LANES), f32),
        pltpu.VMEM((ROWS * blocks, LANES), i32),
        pltpu.VMEM((window, 2 * LANES), bf16),
    ]
    params = pltpu.CompilerParams(vmem_limit_bytes=VMEM_BYTES)
    first = pl.pallas_call(
        first_kernel,
        out_shape=[shape((levels, halo), bf16)] * 2 + held_shapes + result_shapes,
        in_specs=[anywhere] * 6,
        out_specs=[vmem] * 12,
        scratch_shapes=[
            pltpu.VMEM((2, halo), i32),
            pltpu.VMEM((edges // 256 * 64, 256), bf16),
            pltpu.VMEM((edges // 256 * 64, 2 * halo), f32),
        ]
        + work
        + [pltpu.SemaphoreType.DMA((1 + PIECES + 4,))],
        compiler_params=params,
        name="first_cells",
    )(
        *[
            pltpu.with_memory_space_constraint(array, pltpu.HBM)
            for array in (
                send_edges,
                edge_wind,
                stencil,
                rbf_rows,
                state_rows,
                rain_cols.reshape(1, slots),
            )
        ],
    )
    toward_left, toward_right = first[:2]
    held, results = first[2:7], first[7:]
    count = lax.axis_size("dom")
    from_left = lax.ppermute(toward_right, "dom", [(i, (i + 1) % count) for i in range(count)])
    from_right = lax.ppermute(toward_left, "dom", [((i + 1) % count, i) for i in range(count)])
    tend, _, wide, part, edge_table, mask = pl.pallas_call(
        second_kernel,
        out_shape=result_shapes + [shape((blocks, LANES), f32)],
        in_specs=[vmem] * 5 + [pl.BlockSpec(memory_space=pltpu.SMEM)] + [vmem] * 6,
        out_specs=[vmem] * 6,
        scratch_shapes=work,
        input_output_aliases={7 + n: n for n in range(5)},
        compiler_params=params,
        name="second_cells",
    )(*held, rain_count, from_left, *results)
    tend, wind, _, _ = pl.pallas_call(
        outer_kernel,
        out_shape=[
            shape((levels, blocks * 4, LANES), f32),
            shape((levels * blocks * 2, LANES), bf16),
            result_shapes[0],
            result_shapes[2],
        ],
        in_specs=[vmem] * 7,
        out_specs=[anywhere] * 2 + [vmem] * 2,
        scratch_shapes=[
            pltpu.VMEM((levels * blocks * 2, LANES), bf16),
            pltpu.SemaphoreType.DMA((3,)),
        ],
        input_output_aliases={5: 2, 6: 3},
        compiler_params=params,
        name="outer_cells",
    )(from_right, part, edge_table, mask, held[3], tend, wide)
    tendency = jnp.transpose(tend.reshape(levels, blocks, 4, LANES), (2, 0, 1, 3)).reshape(
        4, levels, cells
    )
    cell_wind = jnp.transpose(wind.reshape(levels, blocks, 2, LANES), (2, 0, 1, 3)).reshape(
        2, levels, cells
    )
    return (cell_wind, tendency)


def solution(mesh):
    placed = (
        P(None, ("dom", "bal")),
        P(None, ("dom", "bal")),
        P(None, ("dom", "bal")),
        P(None, None, ("dom", "bal")),
        P(None, None, ("dom", "bal")),
        P(("dom", "bal")),
        P(("dom", "bal")),
    )
    return jax.shard_map(
        local,
        mesh=mesh,
        in_specs=placed,
        out_specs=(P(None, None, ("dom", "bal")), P(None, None, ("dom", "bal"))),
        check_vma=False,
    )
```

```python
import math

import jax
import jax.numpy as jnp
from jax import lax
from jax.experimental import pallas as pl
from jax.experimental.pallas import tpu as pltpu
from jax.sharding import PartitionSpec as P

NSUB = 3
LOG2E = math.log2(math.e)
LANES = 128
ROWS = 16
PIECES = 1
VMEM_BYTES = 40 * 1024 * 1024
RING = 8


def pick_sends(send_ref, edge_ref, arrivals, left_ref, right_ref, stack_ref, found_ref):
    edges = edge_ref.shape[1]
    width = send_ref.shape[1]
    chunk = 256
    span = edges // len(arrivals)
    wanted = jnp.concatenate([send_ref[0:1, :], send_ref[1:2, :]], axis=1)
    low = jnp.broadcast_to(lax.rem(wanted, chunk), (ROWS, 2 * width)).astype(jnp.int16)
    high = jnp.broadcast_to(wanted // chunk, (8, 2 * width))
    rows = lax.broadcasted_iota(jnp.int32, (ROWS, 2 * width), 0)
    picker = jnp.concatenate(
        [
            jnp.where(low == (rows + row).astype(jnp.int16), jnp.bfloat16(1), jnp.bfloat16(0))
            for row in range(0, chunk, ROWS)
        ],
        axis=0,
    )
    levels = edge_ref.shape[0]
    step = stack_ref.shape[0] // (edges // chunk)
    for first in range(0, edges, chunk):
        if first % span == 0:
            arrivals[first // span].wait()
        base = first // chunk * step
        stack_ref[base : base + levels, :] = edge_ref[:, first : first + chunk]
    found_ref[...] = jnp.dot(stack_ref[...], picker, preferred_element_type=jnp.float32)
    here = [high == n for n in range(edges // chunk)]
    total = []
    for base in range(0, levels, 8):
        some = found_ref[base : base + 8, :]
        for n in range(1, edges // chunk):
            some = jnp.where(here[n], found_ref[n * step + base : n * step + base + 8, :], some)
        total.append(some)
    total = jnp.concatenate(total, axis=0)[:levels].astype(jnp.bfloat16)
    left_ref[...] = total[:, :width]
    right_ref[...] = total[:, width:]


def listed_mask(cols_ref, count):
    slots = cols_ref.shape[1]
    cols = cols_ref[...]
    live = lax.broadcasted_iota(jnp.int32, (1, slots), 1) < count
    high = jnp.where(live, cols // LANES, -1)
    low = lax.rem(cols, LANES)
    rows = jnp.where(lax.broadcasted_iota(jnp.int32, (8, slots), 0) == high, 1.0, 0.0)
    lanes = jnp.where(lax.broadcasted_iota(jnp.int32, (LANES, slots), 0) == low, 1.0, 0.0)
    return lax.dot_general(
        rows.astype(jnp.bfloat16),
        lanes.astype(jnp.bfloat16),
        (((1,), (1,)), ((), ())),
        preferred_element_type=jnp.float32,
    )


def merge_members(sten_ref, rbf_ref, pos_ref, zon_ref, mer_ref, tmp_ref, fold):
    members = sten_ref.shape[0]
    blocks = sten_ref.shape[1] // LANES
    for k in range(blocks):
        tmp_ref[ROWS * k : ROWS * k + members, :] = (
            sten_ref[:, LANES * k : LANES * (k + 1)] - 3 * LANES * k
        )
    places, zonal, merid = [], [], []
    for s in range(members):
        places.append(tmp_ref[pl.ds(s, blocks, stride=ROWS), :])
        zonal.append(rbf_ref[pl.ds(2 * blocks * s, blocks, stride=2), :])
        merid.append(rbf_ref[pl.ds(2 * blocks * s + 1, blocks, stride=2), :])
    for t in range(members):
        z, m = zonal[t], merid[t]
        for s in range(t):
            same = places[s] == places[t]
            z = z + jnp.where(same, zonal[s], 0.0)
            m = m + jnp.where(same, merid[s], 0.0)
        rows = slice(blocks * t, blocks * (t + 1))
        pos_ref[rows, :] = jnp.where(places[t] >= fold, places[t] - fold, places[t])
        zon_ref[rows, :] = z
        mer_ref[rows, :] = m


def build_table(k, members, blocks, fold, window, pos_ref, zon_ref, mer_ref, table_ref):
    def spread(ref, s, kind):
        row = ref[pl.ds(blocks * s + k, 1), :]
        return jnp.broadcast_to(row, (ROWS, LANES)).astype(kind)

    places = [spread(pos_ref, s, jnp.int16) for s in range(members)]
    zonal = [spread(zon_ref, s, jnp.bfloat16) for s in range(members)]
    merid = [spread(mer_ref, s, jnp.bfloat16) for s in range(members)]
    rows = lax.broadcasted_iota(jnp.int32, (ROWS, LANES), 0)
    first = (3 * lax.broadcasted_iota(jnp.int32, (ROWS, LANES), 1)).astype(jnp.int16)
    none = jnp.zeros((ROWS, LANES), jnp.bfloat16)
    for row in range(0, fold, ROWS):
        here = (rows + row).astype(jnp.int16)
        z, m = none, none
        for s in range(members):
            hit = places[s] == here
            z = jnp.where(hit, zonal[s], z)
            m = jnp.where(hit, merid[s], m)
        if row + fold < window:
            low = first <= here
            table_ref[row : row + ROWS, :LANES] = jnp.where(low, z, none)
            table_ref[row : row + ROWS, LANES:] = jnp.where(low, m, none)
            table_ref[fold + row : fold + row + ROWS, :LANES] = jnp.where(low, none, z)
            table_ref[fold + row : fold + row + ROWS, LANES:] = jnp.where(low, none, m)
        else:
            table_ref[row : row + ROWS, :LANES] = z
            table_ref[row : row + ROWS, LANES:] = m


def keep_wind(k, levels, blocks, wind, wide_ref):
    for base in range(0, levels, 8):
        count = min(8, levels - base)
        for c in range(2):
            wide_ref[pl.ds(2 * (blocks * base + k) + c, count, stride=2 * blocks), :] = wind[
                base : base + count, LANES * c : LANES * (c + 1)
            ]


def rain_column(k, levels, blocks, listed, wind, state_ref, tend_ref, dry_ref):
    if listed is not None:
        listed = jnp.broadcast_to(listed, (8, LANES)) > 0.5
    falloff = math.exp(-1.0 / levels)
    stride = 4 * blocks
    above = [None] * NSUB
    for base in reversed(range(0, levels, 8)):
        count = min(8, levels - base)
        u = wind[base : base + count, :LANES]
        v = wind[base : base + count, LANES:]
        airspeed = jnp.sqrt(u * u + v * v + 1.0)
        factor = 0.3 + 0.075 * airspeed
        before = [
            state_ref[pl.ds(stride * base + 4 * k + f, count, stride=stride), :] for f in range(4)
        ]
        t, qv, qc, qr = before
        qvs = jnp.exp2((0.3 * LOG2E) * t)
        cond = jnp.maximum((qv - qvs) / (1.0 + 0.45 * qvs), -qc)
        t, qv, qc = t + 0.8 * cond, qv - cond, qc + cond
        adjusted = (t, qv, qc, qr)
        level = (lax.broadcasted_iota(jnp.int32, (count, LANES), 0) + base).astype(jnp.float32)
        height = level * (LOG2E / levels) - 1.0
        for substep in range(NSUB):
            qvs = jnp.exp2((0.3 * LOG2E) * t)
            log_rain = jnp.log2(qr)
            collected = 0.5 * jnp.maximum(qc - 0.5, 0.0) + 1.5 * qc * jnp.exp2(0.875 * log_rain)
            sink = jnp.minimum(collected, qc)
            evap = factor * jnp.maximum(qvs - qv, 0.0) * jnp.exp2(0.525 * log_rain)
            evap = jnp.minimum(evap, qr)
            t = t - 0.8 * evap
            qv = qv + evap
            qc = qc - sink
            mid = (qr + sink) - evap
            fall = jnp.minimum(jnp.exp2(0.1364 * jnp.log2(mid) + height), 0.9) * mid
            top = above[substep]
            if top is None:
                top = jnp.zeros((1, LANES), jnp.float32)
            inflow = jnp.concatenate([fall[1:], top], axis=0)
            above[substep] = fall[:1]
            qr = (mid - fall) + falloff * inflow
        rained = (t, qv, qc, qr)
        for f in range(4):
            rows = pl.ds(stride * base + 4 * k + f, count, stride=stride)
            if listed is None:
                tend_ref[rows, :] = rained[f] - before[f]
                dry_ref[rows, :] = adjusted[f] - before[f]
            else:
                after = jnp.where(listed[:count], rained[f], adjusted[f])
                tend_ref[rows, :] = after - before[f]


def inner_cells(
    edge_ref,
    sten_ref,
    rbf_ref,
    state_ref,
    tend_ref,
    dry_ref,
    wide_ref,
    part_ref,
    edge_table_ref,
    pos_ref,
    zon_ref,
    mer_ref,
    tmp_ref,
    table_ref,
):
    levels, edges = edge_ref.shape
    members, cells = sten_ref.shape
    blocks = cells // LANES
    halo = edge_table_ref.shape[1]
    window = table_ref.shape[0]
    fold = 2 * halo + ROWS
    tend_rows = tend_ref.reshape(tend_ref.shape[0] * 4 * blocks, LANES)
    dry_rows = dry_ref.reshape(dry_ref.shape[0] * 4 * blocks, LANES)
    merge_members(sten_ref, rbf_ref, pos_ref, zon_ref, mer_ref, tmp_ref, fold)

    def table(k):
        build_table(k, members, blocks, fold, window, pos_ref, zon_ref, mer_ref, table_ref)

    def inside(k, carry):
        table(k)
        start = pl.multiple_of(3 * LANES * k - halo, LANES)
        wind = jnp.dot(
            edge_ref[:, pl.ds(start, window)], table_ref[...], preferred_element_type=jnp.float32
        )
        keep_wind(k, levels, blocks, wind, wide_ref)
        rain_column(k, levels, blocks, None, wind, state_ref, tend_rows, dry_rows)
        return carry

    lax.fori_loop(1, blocks - 1, inside, 0)

    def border(side, carry):
        table(side * (blocks - 1))
        keep = pl.multiple_of(side * (window - halo), LANES)
        rest = pl.multiple_of((1 - side) * halo, LANES)
        start = pl.multiple_of(side * (edges - window + halo), LANES)
        edge_table_ref[side] = table_ref[pl.ds(keep, halo), :]
        part_ref[side] = jnp.dot(
            edge_ref[:, pl.ds(start, window - halo)],
            table_ref[pl.ds(rest, window - halo), :],
            preferred_element_type=jnp.float32,
        )
        return carry

    lax.fori_loop(0, 2, border, 0)


def is_early():
    dom, bal = lax.axis_index("dom"), lax.axis_index("bal")
    return jnp.logical_and(lax.rem(dom, RING) == 0, dom + bal > 0)


def is_latest():
    return lax.rem(lax.axis_index("dom"), RING) == RING - 1


def fetches(sources, targets, sem, base):
    return [
        pltpu.make_async_copy(source, target.at[pl.ds(0, source.shape[0])], sem.at[base + n])
        for n, (source, target) in enumerate(zip(sources, targets))
    ]


def first_kernel(*refs):
    sources, refs = refs[:6], refs[6:]
    left_ref, right_ref = refs[:2]
    held, results, refs = refs[2:7], refs[7:12], refs[12:]
    send_ref, work, sem = refs[0], refs[3:8], refs[8]
    edge_in, rest_in = sources[1], sources[2:]
    edge_ref = held[0]
    edges = edge_ref.shape[1]
    span = edges // PIECES
    arrivals = []
    for piece in range(PIECES):
        part = pl.ds(piece * span, span)
        arrivals.append(
            pltpu.make_async_copy(edge_in.at[:, part], edge_ref.at[:, part], sem.at[1 + piece])
        )
        arrivals[-1].start()
    first = pltpu.make_async_copy(sources[0], send_ref, sem.at[0])
    first.start()
    others = fetches(rest_in, held[1:], sem, 1 + PIECES)

    @pl.when(jnp.logical_not(is_latest()))
    def _():
        for copy in others:
            copy.start()

    first.wait()
    pick_sends(send_ref, edge_ref, arrivals, left_ref, right_ref, *refs[1:3])

    @pl.when(jnp.logical_not(is_latest()))
    def _():
        for copy in others:
            copy.wait()

    @pl.when(is_early())
    def _():
        inner_cells(*held[:4], *results, *work)


def second_kernel(*refs):
    edge_ref, count_ref, left_ref, sources, refs = refs[0], refs[1], refs[2], refs[3:7], refs[16:]
    results, mask_ref, held, refs = refs[:5], refs[5], (edge_ref, *refs[6:10]), refs[10:]
    work, sem = refs[:5], refs[5]
    tend_ref, dry_ref, wide_ref, part_ref, edge_table_ref = results
    levels = left_ref.shape[0]
    blocks = mask_ref.shape[0]
    others = fetches(sources, held[1:], sem, 0)

    @pl.when(is_latest())
    def _():
        for copy in others:
            copy.start()
        for copy in others:
            copy.wait()

    @pl.when(jnp.logical_not(is_early()))
    def _():
        inner_cells(*held[:4], *results, *work)

    mask = listed_mask(held[4], count_ref[0])
    mask_ref[...] = mask
    group = 8
    fields = group // 2
    listed = [
        jnp.concatenate(
            [
                jnp.broadcast_to(mask[k : k + 1], (fields, LANES)),
                jnp.broadcast_to(mask[k + 1 : k + 2], (fields, LANES)),
            ],
            axis=0,
        )
        > 0.5
        for k in range(0, blocks, 2)
    ]

    def choose(level, carry):
        for n, here in enumerate(listed):
            rows = slice(group * n, group * (n + 1))
            tend_ref[level, rows] = jnp.where(here, tend_ref[level, rows], dry_ref[level, rows])
        return carry

    lax.fori_loop(0, levels, choose, 0, unroll=5)
    wind = part_ref[0] + jnp.dot(
        left_ref[...], edge_table_ref[0], preferred_element_type=jnp.float32
    )
    tend_rows = tend_ref.reshape(tend_ref.shape[0] * 4 * blocks, LANES)
    keep_wind(0, levels, blocks, wind, wide_ref)
    rain_column(0, levels, blocks, mask[:1], wind, held[3], tend_rows, None)


def outer_kernel(
    right_ref,
    part_ref,
    edge_table_ref,
    mask_ref,
    state_ref,
    tend_in,
    wide_in,
    tend_out,
    wind_out,
    tend_ref,
    wide_ref,
    wind_ref,
    sem,
):
    del tend_in, wide_in
    levels = right_ref.shape[0]
    blocks = mask_ref.shape[0]
    group = 8
    last = blocks - 1

    def send(first, count, n):
        part = pl.ds(first, count)
        copy = pltpu.make_async_copy(
            tend_ref.at[pl.ds(0, levels), part], tend_out.at[:, part], sem.at[n]
        )
        copy.start()
        return copy

    copies = [send(0, 4 * blocks - group, 0)]
    wind = part_ref[1] + jnp.dot(
        right_ref[...], edge_table_ref[1], preferred_element_type=jnp.float32
    )
    keep_wind(last, levels, blocks, wind, wide_ref)
    for level in range(levels):
        rows = slice(2 * blocks * level, 2 * blocks * (level + 1))
        wind_ref[rows, :] = wide_ref[rows, :].astype(jnp.bfloat16)
    copies.append(pltpu.make_async_copy(wind_ref, wind_out, sem.at[1]))
    copies[-1].start()
    tend_rows = tend_ref.reshape(tend_ref.shape[0] * 4 * blocks, LANES)
    rain_column(last, levels, blocks, mask_ref[last:blocks, :], wind, state_ref, tend_rows, None)
    copies.append(send(4 * blocks - group, group, 2))
    for copy in copies:
        copy.wait()


def local(edge_wind, send_edges, stencil, rbf_coeff, state, rain_cols, rain_count):
    levels, edges = edge_wind.shape
    halo = send_edges.shape[1]
    members, cells = stencil.shape
    blocks = cells // LANES
    slots = rain_cols.shape[0]
    padded = -(-levels // 8) * 8
    window = 3 * LANES + 2 * halo
    vmem = pl.BlockSpec(memory_space=pltpu.VMEM)
    anywhere = pl.BlockSpec(memory_space=pltpu.HBM)
    f32, bf16, i32 = jnp.float32, jnp.bfloat16, jnp.int32
    shape = jax.ShapeDtypeStruct
    state_rows = jnp.transpose(state.reshape(4, levels, blocks, LANES), (1, 2, 0, 3)).reshape(
        levels * blocks * 4, LANES
    )
    rbf_rows = jnp.transpose(rbf_coeff.reshape(2, members, blocks, LANES), (1, 2, 0, 3)).reshape(
        members * blocks * 2, LANES
    )
    held_shapes = [
        shape((levels, edges), bf16),
        shape((members, cells), i32),
        shape((members * blocks * 2, LANES), f32),
        shape((padded * blocks * 4, LANES), f32),
        shape((1, slots), i32),
    ]
    result_shapes = [
        shape((padded, blocks * 4, LANES), f32),
        shape((padded, blocks * 4, LANES), f32),
        shape((padded * blocks * 2, LANES), f32),
        shape((2, levels, 2 * LANES), f32),
        shape((2, halo, 2 * LANES), bf16),
    ]
    work = [
        pltpu.VMEM((members * blocks, LANES), i32),
        pltpu.VMEM((members * blocks, LANES), f32),
        pltpu.VMEM((members * blocks, LANES), f32),
        pltpu.VMEM((ROWS * blocks, LANES), i32),
        pltpu.VMEM((window, 2 * LANES), bf16),
    ]
    params = pltpu.CompilerParams(vmem_limit_bytes=VMEM_BYTES)
    sources = [
        pltpu.with_memory_space_constraint(array, pltpu.HBM)
        for array in (
            send_edges,
            edge_wind,
            stencil,
            rbf_rows,
            state_rows,
            rain_cols.reshape(1, slots),
        )
    ]
    first = pl.pallas_call(
        first_kernel,
        out_shape=[shape((levels, halo), bf16)] * 2 + held_shapes + result_shapes,
        in_specs=[anywhere] * 6,
        out_specs=[vmem] * 12,
        scratch_shapes=[
            pltpu.VMEM((2, halo), i32),
            pltpu.VMEM((edges // 256 * 64, 256), bf16),
            pltpu.VMEM((edges // 256 * 64, 2 * halo), f32),
        ]
        + work
        + [pltpu.SemaphoreType.DMA((1 + PIECES + 4,))],
        compiler_params=params,
        name="first_cells",
    )(*sources)
    toward_left, toward_right = first[:2]
    held, results = first[2:7], first[7:]
    count = lax.axis_size("dom")
    from_left = lax.ppermute(toward_right, "dom", [(i, (i + 1) % count) for i in range(count)])
    from_right = lax.ppermute(toward_left, "dom", [((i + 1) % count, i) for i in range(count)])
    tend, _, wide, part, edge_table, mask, _, _, state_held, _ = pl.pallas_call(
        second_kernel,
        out_shape=result_shapes + [shape((blocks, LANES), f32)] + held_shapes[1:],
        in_specs=[vmem, pl.BlockSpec(memory_space=pltpu.SMEM), vmem] + [anywhere] * 4 + [vmem] * 9,
        out_specs=[vmem] * 10,
        scratch_shapes=work + [pltpu.SemaphoreType.DMA((4,))],
        input_output_aliases={7 + n: 6 + n for n in range(4)} | {11 + n: n for n in range(5)},
        compiler_params=params,
        name="second_cells",
    )(held[0], rain_count, from_left, *sources[2:], *held[1:], *results)
    tend, wind, _, _ = pl.pallas_call(
        outer_kernel,
        out_shape=[
            shape((levels, blocks * 4, LANES), f32),
            shape((levels * blocks * 2, LANES), bf16),
            result_shapes[0],
            result_shapes[2],
        ],
        in_specs=[vmem] * 7,
        out_specs=[anywhere] * 2 + [vmem] * 2,
        scratch_shapes=[
            pltpu.VMEM((levels * blocks * 2, LANES), bf16),
            pltpu.SemaphoreType.DMA((3,)),
        ],
        input_output_aliases={5: 2, 6: 3},
        compiler_params=params,
        name="outer_cells",
    )(from_right, part, edge_table, mask, state_held, tend, wide)
    tendency = jnp.transpose(tend.reshape(levels, blocks, 4, LANES), (2, 0, 1, 3)).reshape(
        4, levels, cells
    )
    cell_wind = jnp.transpose(wind.reshape(levels, blocks, 2, LANES), (2, 0, 1, 3)).reshape(
        2, levels, cells
    )
    return (cell_wind, tendency)


def solution(mesh):
    placed = (
        P(None, ("dom", "bal")),
        P(None, ("dom", "bal")),
        P(None, ("dom", "bal")),
        P(None, None, ("dom", "bal")),
        P(None, None, ("dom", "bal")),
        P(("dom", "bal")),
        P(("dom", "bal")),
    )
    return jax.shard_map(
        local,
        mesh=mesh,
        in_specs=placed,
        out_specs=(P(None, None, ("dom", "bal")), P(None, None, ("dom", "bal"))),
        check_vma=False,
    )
```
